32 devices in a mesh: dp: 4 (over z), expert: 8 (over y, x, core).
Axes of the slice: x: 2, y: 2, z: 4, core: 2. Of those that a mesh axis runs over, the one named last changes fastest.
Arguments:
- x_routed: bfloat16 [8, 512, 2048], P(None, 'dp', 'expert'), may hold values from -10 to 10
- grad_out: bfloat16 [8, 512, 768], P(None, 'dp'), may hold values from -15 to 15
- block_counts: int32 [4, 8], P('dp'), may hold values from 1 to 8, as said below
Outputs:
- update: bfloat16 [8, 2048, 768], P(None, 'expert')
The draws below stay inside these ranges and needn't reach their ends.
Inputs may be any that keep to these rules, and one draw needn't show every extreme that they name: Rows of replica r beyond 16 * block_counts[r, e] of expert e are padding; on every replica one expert has all 128 rows live.
All inputs are finite; a program needn't handle non-finite values.
Results may differ from the reference program's by a relative error of at most 0.0065.
Values may be sent and summed in bfloat16 or wider, within the bound.
A program may use at most 64 MiB of HBM per device.

```python
import math
import jax
import jax.numpy as jnp
from jax import lax

D = 2048
FF = 768
CAP = 128
BLK = 16
ITERS = 2
EXPERTS = 8
REPLICAS = 4


def column_scales(key_cols, number):
    return jnp.exp(jax.random.uniform(key_cols, (number,), jnp.float32, 0.0, math.log(10.0)))


def draw_x_routed(key, part):
    key_base, key_cols = jax.random.split(jax.random.fold_in(key, 11), 2)
    array_shape = (EXPERTS, CAP * REPLICAS, D)
    values_base = jnp.clip(jax.random.normal(key_base, array_shape, jnp.float32), -4.0, 4.0)
    return (values_base * column_scales(key_cols, D)[None, None, :] / 4.0).astype(jnp.bfloat16)


def draw_grad_out(key, part):
    key_base, key_cols = jax.random.split(jax.random.fold_in(key, 23), 2)
    array_shape = (EXPERTS, CAP * REPLICAS, FF)
    replica = (jnp.arange(CAP * REPLICAS) // CAP).astype(jnp.float32)
    rising = 1.0 + 2.0 * replica / max(REPLICAS - 1, 1)
    values_base = jnp.clip(jax.random.normal(key_base, array_shape, jnp.float32), -4.0, 4.0)
    scaled = values_base * rising[None, :, None] * column_scales(key_cols, FF)[None, None, :] / 10.0
    return scaled.astype(jnp.bfloat16)


def draw_block_counts(key, part):
    key_values, key_full = jax.random.split(jax.random.fold_in(key, 37))
    blocks = CAP // BLK
    values_drawn = jax.random.randint(key_values, (REPLICAS, EXPERTS), 1, blocks + 1)
    full_expert = jax.random.randint(key_full, (REPLICAS, 1), 0, EXPERTS)
    expert_index = jnp.arange(EXPERTS)[None, :]
    return jnp.where(expert_index == full_expert, blocks, values_drawn).astype(jnp.int32)


def setup_inputs(seed: int = 0) -> dict:
    keys = jax.random.split(jax.random.key(seed), 4)
    return {
        "x_routed": draw_x_routed(jax.random.fold_in(keys[3], 71), 0),
        "grad_out": draw_grad_out(jax.random.fold_in(keys[3], 71), 0),
        "block_counts": draw_block_counts(jax.random.fold_in(keys[3], 71), 0),
    }


NEWTON_FIRST = 3.4445
NEWTON_SECOND = -4.775
NEWTON_THIRD = 2.0315
EPSILON = 1e-07

def live_rows(block_counts):
    row_index = jnp.arange(CAP * REPLICAS, dtype=jnp.int32)
    within = row_index % CAP
    replica = row_index // CAP
    limit = BLK * block_counts.T[:, replica]
    return within[None, :] < limit

def orthogonal(gradient):
    total = jnp.sum(gradient * gradient)
    current = (gradient / (jnp.sqrt(total) + EPSILON)).astype(jnp.bfloat16)
    for iteration in range(ITERS):
        gram_matrix = lax.dot_general(current, current, (((0,), (0,)), ((), ())), preferred_element_type=jnp.float32).astype(jnp.bfloat16)
        square = jnp.dot(gram_matrix, gram_matrix, preferred_element_type=jnp.float32)
        polynomial = (NEWTON_SECOND * gram_matrix.astype(jnp.float32) + NEWTON_THIRD * square).astype(jnp.bfloat16)
        combined = NEWTON_FIRST * current.astype(jnp.float32) + jnp.dot(current, polynomial, preferred_element_type=jnp.float32)
        if iteration + 1 == ITERS:
            combined = combined * math.sqrt(D)
        current = combined.astype(jnp.bfloat16)
    return current

def one_expert(operands):
    x_expert, grad_expert = operands
    gradient = lax.dot_general(x_expert, grad_expert, (((0,), (0,)), ((), ())), preferred_element_type=jnp.float32)
    return orthogonal(gradient)

def reference(x_routed, grad_out, block_counts):
    live_mask = live_rows(block_counts)
    masked = jnp.where(live_mask[:, :, None], grad_out, jnp.zeros((), grad_out.dtype))
    return lax.map(one_expert, (x_routed, masked))
```

```python
import math

import jax
import jax.numpy as jnp
from jax import lax
from jax.sharding import PartitionSpec as P

D = 2048
BLK = 16
ITERS = 2


NEWTON_FIRST = 3.4445
NEWTON_SECOND = -4.775
NEWTON_THIRD = 2.0315
EPSILON = 1e-07


def newton_turn(current, gram_matrix, final_turn):
    square = jnp.dot(gram_matrix, gram_matrix, preferred_element_type=jnp.float32)
    polynomial = (NEWTON_SECOND * gram_matrix.astype(jnp.float32) + NEWTON_THIRD * square).astype(
        jnp.bfloat16
    )
    combined = NEWTON_FIRST * current.astype(jnp.float32) + jnp.dot(
        current, polynomial, preferred_element_type=jnp.float32
    )
    if final_turn:
        combined = combined * math.sqrt(D)
    return combined.astype(jnp.bfloat16)


def contract_rows(left, right):
    return lax.dot_general(
        left, right, (((0,), (0,)), ((), ())), preferred_element_type=jnp.float32
    )


def per_device(x_routed, grad_out, block_counts):
    slice_width = x_routed.shape[2]
    capacity, hidden_width = grad_out.shape[1:]
    groups = lax.axis_size("expert")
    expert = lax.axis_index("expert")
    x_rows = lax.all_to_all(x_routed, "expert", split_axis=0, concat_axis=2, tiled=True)[0]
    g_rows = lax.dynamic_index_in_dim(grad_out, expert, 0, keepdims=False)
    count = lax.dynamic_index_in_dim(block_counts[0], expert, 0, keepdims=False)
    row_index = lax.broadcasted_iota(jnp.int32, (capacity, 1), 0)
    g_rows = jnp.where(row_index < BLK * count, g_rows, jnp.zeros((), g_rows.dtype))
    g_all = lax.all_gather(g_rows, "dp", axis=0, tiled=True)
    x_all = lax.all_gather(x_rows, "dp", axis=0, tiled=True)
    gradient = contract_rows(x_all, g_all)
    norm_total = jnp.sum(gradient * gradient)
    current = (gradient / (jnp.sqrt(norm_total) + EPSILON)).astype(jnp.bfloat16)
    for iteration in range(ITERS):
        gram_matrix = contract_rows(current, current).astype(jnp.bfloat16)
        current = newton_turn(current, gram_matrix, iteration + 1 == ITERS)
    arranged = current.reshape(groups, slice_width, hidden_width)
    return lax.all_to_all(arranged, "expert", split_axis=0, concat_axis=0, tiled=True)


def solution(mesh):
    return jax.shard_map(
        per_device,
        mesh=mesh,
        in_specs=(P(None, "dp", "expert"), P(None, "dp", None), P("dp", None)),
        out_specs=P(None, "expert", None),
        check_vma=False,
    )
```

```python
import functools
import math

import jax
import jax.numpy as jnp
from jax import lax
from jax.experimental import pallas as pl
from jax.experimental.pallas import tpu as pltpu
from jax.sharding import PartitionSpec as P

D = 2048
BLK = 16
ITERS = 2


NEWTON_FIRST = 3.4445
NEWTON_SECOND = -4.775
NEWTON_THIRD = 2.0315
EPSILON = 1e-07
TILE = 256
MESH = pl.DeviceIdType.MESH


def contract_rows(left, right):
    return lax.dot_general(
        left, right, (((0,), (0,)), ((), ())), preferred_element_type=jnp.float32
    )


def gram_into(gram_ref, rows_ref, scale):
    groups, width, hidden = rows_ref.shape
    for low in range(0, hidden, TILE):
        left = rows_ref[:, :, low : low + TILE].reshape(groups * width, TILE)
        right = rows_ref[:, :, low:].reshape(groups * width, hidden - low)
        strip = contract_rows(left, right)
        if scale is not None:
            strip = strip * scale
        gram_ref[low : low + TILE, low:] = strip.astype(jnp.bfloat16)
        for other in range(low + TILE, hidden, TILE):
            block = strip[:, other - low : other - low + TILE]
            gram_ref[other : other + TILE, low : low + TILE] = block.T.astype(jnp.bfloat16)


def polynomial_into(poly_ref, gram_ref):
    hidden = gram_ref.shape[0]
    for low in range(0, hidden, TILE):
        strip = gram_ref[low : low + TILE, :]
        square = jnp.dot(strip, gram_ref[...], preferred_element_type=jnp.float32)
        poly_ref[low : low + TILE, :] = (
            NEWTON_SECOND * strip.astype(jnp.float32) + NEWTON_THIRD * square
        ).astype(jnp.bfloat16)


def turn(rows, poly_ref):
    return NEWTON_FIRST * rows.astype(jnp.float32) + jnp.dot(
        rows, poly_ref[...], preferred_element_type=jnp.float32
    )


def kernel(
    groups,
    replicas,
    parts,
    counts_ref,
    x_ref,
    g_ref,
    out_ref,
    x_all,
    g_all,
    g_raw,
    grad,
    current,
    stage,
    gram,
    poly,
    local_sem,
    x_send,
    x_recv,
    right_send,
    left_send,
    line_recv,
    out_send,
    out_recv,
):
    z = lax.axis_index("dp")
    me = lax.axis_index("expert")
    capacity = g_raw.shape[0]
    per_part = groups // parts
    last = replicas - 1
    right_exists = z < last
    left_exists = z > 0

    barrier = pltpu.get_barrier_semaphore()

    def greet(step, carry):
        peer = lax.rem(me + step, groups)
        pl.semaphore_signal(barrier, inc=1, device_id=(z, peer), device_id_type=MESH)
        return carry

    lax.fori_loop(1, groups, greet, 0)

    @pl.when(right_exists)
    def _():
        pl.semaphore_signal(barrier, inc=1, device_id=(z + 1, me), device_id_type=MESH)

    @pl.when(left_exists)
    def _():
        pl.semaphore_signal(barrier, inc=1, device_id=(z - 1, me), device_id_type=MESH)

    own_g = pltpu.make_async_copy(g_ref.at[me], g_raw, local_sem.at[0])
    own_g.start()
    own_x = pltpu.make_async_copy(x_ref.at[me], x_all.at[z, me], local_sem.at[1])
    own_x.start()

    neighbours = jnp.minimum(z, 1) + jnp.minimum(last - z, 1)
    pl.semaphore_wait(barrier, groups - 1 + neighbours)

    def x_copy(peer):
        return pltpu.make_async_remote_copy(
            src_ref=x_ref.at[peer],
            dst_ref=x_all.at[z, me],
            send_sem=x_send.at[peer],
            recv_sem=x_recv.at[me],
            device_id=(z, peer),
            device_id_type=MESH,
        )

    def x_arrival(peer):
        return pltpu.make_async_remote_copy(
            src_ref=x_ref.at[peer],
            dst_ref=x_all.at[z, peer],
            send_sem=x_send.at[peer],
            recv_sem=x_recv.at[peer],
            device_id=(z, peer),
            device_id_type=MESH,
        )

    def exchange(step, carry):
        x_copy(lax.rem(me + step, groups)).start()
        return carry

    lax.fori_loop(1, groups, exchange, 0)

    def line_copy(block, part, to, send_sem):
        if part == 0:
            view = g_all.at[block]
        else:
            view = x_all.at[block, pl.ds((part - 1) * per_part, per_part)]
        return pltpu.make_async_remote_copy(
            src_ref=view,
            dst_ref=view,
            send_sem=send_sem.at[block, part],
            recv_sem=line_recv.at[block, part],
            device_id=(to, me),
            device_id_type=MESH,
        )

    def to_right(block, part):
        return line_copy(block, part, z + 1, right_send)

    def to_left(block, part):
        return line_copy(block, part, z - 1, left_send)

    own_g.wait()
    row_index = lax.broadcasted_iota(jnp.int32, g_raw.shape, 0)
    live = row_index < BLK * counts_ref[0, me]
    g_all[z] = jnp.where(live, g_raw[...], jnp.zeros((), g_raw.dtype))

    for part in range(parts + 1):
        if part > 0:
            for peer in range((part - 1) * per_part, part * per_part):

                @pl.when(me == peer)
                def _():
                    own_x.wait()

                @pl.when(me != peer)
                def _():
                    x_arrival(peer).wait_recv()

        @pl.when(right_exists)
        def _():
            to_right(z, part).start()

        @pl.when(left_exists)
        def _():
            to_left(z, part).start()

    for step in range(1, replicas):
        for part in range(parts + 1):

            @pl.when(z >= step)
            def _():
                to_right(z - step, part).wait_recv()

                @pl.when(right_exists)
                def _():
                    to_right(z - step, part).start()

            @pl.when(z + step <= last)
            def _():
                to_left(z + step, part).wait_recv()

                @pl.when(left_exists)
                def _():
                    to_left(z + step, part).start()

    hidden = g_raw.shape[1]
    width = x_ref.shape[2]
    rows = replicas * capacity

    def gradient(group, total):
        block = contract_rows(
            x_all[:, group].reshape(rows, width), g_all[...].reshape(rows, hidden)
        )
        grad[group] = block.astype(jnp.bfloat16)
        return total + jnp.sum((block * block).reshape(width // 8, 8, hidden), axis=0)

    total = lax.fori_loop(0, groups, gradient, jnp.zeros((8, hidden), jnp.float32))
    norm = jnp.sqrt(jnp.sum(total, keepdims=True)) + EPSILON
    scale = 1.0 / norm
    gram_into(gram, grad, scale * scale)
    for iteration in range(ITERS - 1):
        source = grad if iteration == 0 else current
        polynomial_into(poly, gram)

        def advance(group, carry):
            combined = turn(source[group], poly)
            if iteration == 0:
                combined = combined * scale
            current[group] = combined.astype(jnp.bfloat16)
            return carry

        lax.fori_loop(0, groups, advance, 0)
        gram_into(gram, current, None)
    polynomial_into(poly, gram)

    def out_copy(peer):
        return pltpu.make_async_remote_copy(
            src_ref=stage.at[peer],
            dst_ref=out_ref.at[me],
            send_sem=out_send.at[peer],
            recv_sem=out_recv.at[me],
            device_id=(z, peer),
            device_id_type=MESH,
        )

    def out_arrival(peer):
        return pltpu.make_async_remote_copy(
            src_ref=stage.at[peer],
            dst_ref=out_ref.at[peer],
            send_sem=out_send.at[peer],
            recv_sem=out_recv.at[peer],
            device_id=(z, peer),
            device_id_type=MESH,
        )

    def finish(peer):
        stage[peer] = (turn(current[peer], poly) * math.sqrt(D)).astype(jnp.bfloat16)

    def send_out(step, carry):
        peer = lax.rem(me + step, groups)
        finish(peer)
        out_copy(peer).start()
        return carry

    lax.fori_loop(1, groups, send_out, 0)
    finish(me)
    own_out = pltpu.make_async_copy(stage.at[me], out_ref.at[me], local_sem.at[0])
    own_out.start()

    def settle(step, carry):
        peer = lax.rem(me + step, groups)
        x_copy(peer).wait_send()
        out_copy(peer).wait_send()
        out_arrival(peer).wait_recv()
        return carry

    lax.fori_loop(1, groups, settle, 0)
    own_out.wait()
    for step in range(replicas):
        for part in range(parts + 1):

            @pl.when(jnp.logical_and(z >= step, right_exists))
            def _():
                to_right(z - step, part).wait_send()

            @pl.when(jnp.logical_and(z + step <= last, left_exists))
            def _():
                to_left(z + step, part).wait_send()


def per_device(x_routed, grad_out, block_counts):
    groups = lax.axis_size("expert")
    replicas = lax.axis_size("dp")
    experts, capacity, width = x_routed.shape
    hidden = grad_out.shape[2]
    parts = 4
    dma = pltpu.SemaphoreType.DMA
    return pl.pallas_call(
        functools.partial(kernel, groups, replicas, parts),
        out_shape=jax.ShapeDtypeStruct((groups, width, hidden), jnp.bfloat16),
        in_specs=[
            pl.BlockSpec(memory_space=pltpu.SMEM),
            pl.BlockSpec(memory_space=pl.ANY),
            pl.BlockSpec(memory_space=pl.ANY),
        ],
        out_specs=pl.BlockSpec(memory_space=pl.ANY),
        scratch_shapes=[
            pltpu.VMEM((replicas, groups, capacity, width), jnp.bfloat16),
            pltpu.VMEM((replicas, capacity, hidden), jnp.bfloat16),
            pltpu.VMEM((capacity, hidden), jnp.bfloat16),
            pltpu.VMEM((groups, width, hidden), jnp.bfloat16),
            pltpu.VMEM((groups, width, hidden), jnp.bfloat16),
            pltpu.VMEM((groups, width, hidden), jnp.bfloat16),
            pltpu.VMEM((hidden, hidden), jnp.bfloat16),
            pltpu.VMEM((hidden, hidden), jnp.bfloat16),
            dma((2,)),
            dma((groups,)),
            dma((groups,)),
            dma((replicas, parts + 1)),
            dma((replicas, parts + 1)),
            dma((replicas, parts + 1)),
            dma((groups,)),
            dma((groups,)),
        ],
        compiler_params=pltpu.CompilerParams(
            collective_id=0, has_side_effects=True, vmem_limit_bytes=56 * 2**20
        ),
    )(block_counts, x_routed, grad_out)


def solution(mesh):
    return jax.shard_map(
        per_device,
        mesh=mesh,
        in_specs=(P(None, "dp", "expert"), P(None, "dp", None), P("dp", None)),
        out_specs=P(None, "expert", None),
        check_vma=False,
    )
```

```python
import functools
import math

import jax
import jax.numpy as jnp
from jax import lax
from jax.experimental import pallas as pl
from jax.experimental.pallas import tpu as pltpu
from jax.sharding import PartitionSpec as P

D = 2048
BLK = 16
ITERS = 2


NEWTON_FIRST = 3.4445
NEWTON_SECOND = -4.775
NEWTON_THIRD = 2.0315
EPSILON = 1e-07
TILE = 256
MESH = pl.DeviceIdType.MESH


def contract_rows(left, right):
    return lax.dot_general(
        left, right, (((0,), (0,)), ((), ())), preferred_element_type=jnp.float32
    )


def gram_into(gram_ref, rows_ref, scale):
    groups, width, hidden = rows_ref.shape
    for low in range(0, hidden, TILE):
        left = rows_ref[:, :, low : low + TILE].reshape(groups * width, TILE)
        right = rows_ref[:, :, low:].reshape(groups * width, hidden - low)
        strip = contract_rows(left, right)
        if scale is not None:
            strip = strip * scale
        gram_ref[low : low + TILE, low:] = strip.astype(jnp.bfloat16)
        for other in range(low + TILE, hidden, TILE):
            block = strip[:, other - low : other - low + TILE]
            gram_ref[other : other + TILE, low : low + TILE] = block.T.astype(jnp.bfloat16)


def polynomial_into(poly_ref, gram_ref):
    hidden = gram_ref.shape[0]
    for low in range(0, hidden, TILE):
        strip = gram_ref[low : low + TILE, :]
        square = jnp.dot(strip, gram_ref[...], preferred_element_type=jnp.float32)
        poly_ref[low : low + TILE, :] = (
            NEWTON_SECOND * strip.astype(jnp.float32) + NEWTON_THIRD * square
        ).astype(jnp.bfloat16)


def turn(rows, poly_ref):
    return NEWTON_FIRST * rows.astype(jnp.float32) + jnp.dot(
        rows, poly_ref[...], preferred_element_type=jnp.float32
    )


def kernel(
    groups,
    replicas,
    parts,
    counts_ref,
    x_ref,
    g_ref,
    out_ref,
    x_all,
    g_all,
    g_raw,
    grad,
    current,
    stage,
    gram,
    poly,
    local_sem,
    x_send,
    x_recv,
    right_send,
    left_send,
    line_recv,
    out_send,
    out_recv,
    handed,
):
    z = lax.axis_index("dp")
    me = lax.axis_index("expert")
    capacity = g_raw.shape[0]
    per_part = groups // parts
    last = replicas - 1
    right_exists = z < last
    left_exists = z > 0

    barrier = pltpu.get_barrier_semaphore()

    def greet(step, carry):
        peer = lax.rem(me + step, groups)
        pl.semaphore_signal(barrier, inc=1, device_id=(z, peer), device_id_type=MESH)
        return carry

    lax.fori_loop(1, groups, greet, 0)

    @pl.when(right_exists)
    def _():
        pl.semaphore_signal(barrier, inc=1, device_id=(z + 1, me), device_id_type=MESH)

    @pl.when(left_exists)
    def _():
        pl.semaphore_signal(barrier, inc=1, device_id=(z - 1, me), device_id_type=MESH)

    own_g = pltpu.make_async_copy(g_ref.at[me], g_raw, local_sem.at[0])
    own_g.start()
    own_x = pltpu.make_async_copy(x_ref.at[me], x_all.at[z, me], local_sem.at[1])
    own_x.start()

    neighbours = jnp.minimum(z, 1) + jnp.minimum(last - z, 1)
    pl.semaphore_wait(barrier, groups - 1 + neighbours)

    def x_copy(peer):
        return pltpu.make_async_remote_copy(
            src_ref=x_ref.at[peer],
            dst_ref=x_all.at[z, me],
            send_sem=x_send.at[peer],
            recv_sem=x_recv.at[me],
            device_id=(z, peer),
            device_id_type=MESH,
        )

    def x_arrival(peer):
        return pltpu.make_async_remote_copy(
            src_ref=x_ref.at[peer],
            dst_ref=x_all.at[z, peer],
            send_sem=x_send.at[peer],
            recv_sem=x_recv.at[peer],
            device_id=(z, peer),
            device_id_type=MESH,
        )

    def exchange(step, carry):
        x_copy(lax.rem(me + step, groups)).start()
        return carry

    lax.fori_loop(1, groups, exchange, 0)

    def chunk(part):
        return lax.rem(me // per_part + part - 1, parts)

    def line_copy(block, part, to, send_sem):
        if part == 0:
            view = g_all.at[block]
        else:
            view = x_all.at[block, pl.ds(chunk(part) * per_part, per_part)]
        return pltpu.make_async_remote_copy(
            src_ref=view,
            dst_ref=view,
            send_sem=send_sem.at[block, part],
            recv_sem=line_recv.at[block, part],
            device_id=(to, me),
            device_id_type=MESH,
        )

    def to_right(block, part):
        return line_copy(block, part, z + 1, right_send)

    def to_left(block, part):
        return line_copy(block, part, z - 1, left_send)

    own_g.wait()
    row_index = lax.broadcasted_iota(jnp.int32, g_raw.shape, 0)
    live = row_index < BLK * counts_ref[0, me]
    g_all[z] = jnp.where(live, g_raw[...], jnp.zeros((), g_raw.dtype))

    even = lax.rem(me, 2) == 0
    odd = jnp.logical_not(even)
    low_half = 2 * z < replicas

    def take_link(direction, exists):
        @pl.when(jnp.logical_and(odd, exists))
        def _():
            pl.semaphore_wait(handed.at[direction], 1)

    def give_link(direction, exists):
        @pl.when(jnp.logical_and(even, exists))
        def _():
            pl.semaphore_signal(
                handed.at[direction], inc=1, device_id=(z, me + 1), device_id_type=MESH
            )

    def start_right():
        take_link(0, right_exists)
        for part in range(parts + 1):

            @pl.when(right_exists)
            def _():
                to_right(z, part).start()

    def start_left():
        take_link(1, left_exists)
        for part in range(parts + 1):

            @pl.when(left_exists)
            def _():
                to_left(z, part).start()

    def own_chunk(part):
        for offset in range(per_part):
            peer = chunk(part) * per_part + offset

            @pl.when(me == peer)
            def _():
                own_x.wait()

            @pl.when(me != peer)
            def _():
                x_arrival(peer).wait_recv()

    @pl.when(even)
    def _():
        for part in range(parts + 1):
            if part > 0:
                own_chunk(part)

            @pl.when(right_exists)
            def _():
                to_right(z, part).start()

            @pl.when(left_exists)
            def _():
                to_left(z, part).start()

    @pl.when(odd)
    def _():
        for part in range(1, parts + 1):
            own_chunk(part)

        @pl.when(low_half)
        def _():
            start_right()
            start_left()

        @pl.when(jnp.logical_not(low_half))
        def _():
            start_left()
            start_right()

    for step in range(1, replicas):
        for part in range(parts + 1):

            @pl.when(z >= step)
            def _():
                to_right(z - step, part).wait_recv()

                @pl.when(right_exists)
                def _():
                    to_right(z - step, part).start()

            @pl.when(z + step <= last)
            def _():
                to_left(z + step, part).wait_recv()

                @pl.when(left_exists)
                def _():
                    to_left(z + step, part).start()

    def sent_right(step, part):
        @pl.when(jnp.logical_and(z >= step, right_exists))
        def _():
            to_right(z - step, part).wait_send()

    def sent_left(step, part):
        @pl.when(jnp.logical_and(z + step <= last, left_exists))
        def _():
            to_left(z + step, part).wait_send()

    def release_right():
        for step in range(replicas):
            for part in range(parts):
                sent_right(step, part)
        give_link(0, right_exists)

    def release_left():
        for step in range(replicas):
            for part in range(parts):
                sent_left(step, part)
        give_link(1, left_exists)

    @pl.when(jnp.logical_and(even, low_half))
    def _():
        release_right()
        release_left()

    @pl.when(jnp.logical_and(even, jnp.logical_not(low_half)))
    def _():
        release_left()
        release_right()

    hidden = g_raw.shape[1]
    width = x_ref.shape[2]
    rows = replicas * capacity

    def gradient(group, total):
        block = contract_rows(
            x_all[:, group].reshape(rows, width), g_all[...].reshape(rows, hidden)
        )
        grad[group] = block.astype(jnp.bfloat16)
        return total + jnp.sum((block * block).reshape(width // 8, 8, hidden), axis=0)

    total = lax.fori_loop(0, groups, gradient, jnp.zeros((8, hidden), jnp.float32))
    norm = jnp.sqrt(jnp.sum(total, keepdims=True)) + EPSILON
    scale = 1.0 / norm
    gram_into(gram, grad, scale * scale)
    for iteration in range(ITERS - 1):
        source = grad if iteration == 0 else current
        polynomial_into(poly, gram)

        def advance(group, carry):
            combined = turn(source[group], poly)
            if iteration == 0:
                combined = combined * scale
            current[group] = combined.astype(jnp.bfloat16)
            return carry

        lax.fori_loop(0, groups, advance, 0)
        gram_into(gram, current, None)
    polynomial_into(poly, gram)

    def out_copy(peer):
        return pltpu.make_async_remote_copy(
            src_ref=stage.at[peer],
            dst_ref=out_ref.at[me],
            send_sem=out_send.at[peer],
            recv_sem=out_recv.at[me],
            device_id=(z, peer),
            device_id_type=MESH,
        )

    def out_arrival(peer):
        return pltpu.make_async_remote_copy(
            src_ref=stage.at[peer],
            dst_ref=out_ref.at[peer],
            send_sem=out_send.at[peer],
            recv_sem=out_recv.at[peer],
            device_id=(z, peer),
            device_id_type=MESH,
        )

    def finish(peer):
        stage[peer] = (turn(current[peer], poly) * math.sqrt(D)).astype(jnp.bfloat16)

    def send_out(step, carry):
        peer = lax.rem(me + step, groups)
        finish(peer)
        out_copy(peer).start()
        return carry

    lax.fori_loop(1, groups, send_out, 0)
    finish(me)
    own_out = pltpu.make_async_copy(stage.at[me], out_ref.at[me], local_sem.at[0])
    own_out.start()

    def settle(step, carry):
        peer = lax.rem(me + step, groups)
        x_copy(peer).wait_send()
        out_copy(peer).wait_send()
        out_arrival(peer).wait_recv()
        return carry

    lax.fori_loop(1, groups, settle, 0)
    own_out.wait()

    @pl.when(odd)
    def _():
        for step in range(replicas):
            for part in range(parts):
                sent_right(step, part)
                sent_left(step, part)

    for step in range(replicas):
        sent_right(step, parts)
        sent_left(step, parts)


def per_device(x_routed, grad_out, block_counts):
    groups = lax.axis_size("expert")
    replicas = lax.axis_size("dp")
    experts, capacity, width = x_routed.shape
    hidden = grad_out.shape[2]
    parts = 4
    dma = pltpu.SemaphoreType.DMA
    return pl.pallas_call(
        functools.partial(kernel, groups, replicas, parts),
        out_shape=jax.ShapeDtypeStruct((groups, width, hidden), jnp.bfloat16),
        in_specs=[
            pl.BlockSpec(memory_space=pltpu.SMEM),
            pl.BlockSpec(memory_space=pl.ANY),
            pl.BlockSpec(memory_space=pl.ANY),
        ],
        out_specs=pl.BlockSpec(memory_space=pl.ANY),
        scratch_shapes=[
            pltpu.VMEM((replicas, groups, capacity, width), jnp.bfloat16),
            pltpu.VMEM((replicas, capacity, hidden), jnp.bfloat16),
            pltpu.VMEM((capacity, hidden), jnp.bfloat16),
            pltpu.VMEM((groups, width, hidden), jnp.bfloat16),
            pltpu.VMEM((groups, width, hidden), jnp.bfloat16),
            pltpu.VMEM((groups, width, hidden), jnp.bfloat16),
            pltpu.VMEM((hidden, hidden), jnp.bfloat16),
            pltpu.VMEM((hidden, hidden), jnp.bfloat16),
            dma((2,)),
            dma((groups,)),
            dma((groups,)),
            dma((replicas, parts + 1)),
            dma((replicas, parts + 1)),
            dma((replicas, parts + 1)),
            dma((groups,)),
            dma((groups,)),
            pltpu.SemaphoreType.REGULAR((2,)),
        ],
        compiler_params=pltpu.CompilerParams(
            collective_id=0, has_side_effects=True, vmem_limit_bytes=56 * 2**20
        ),
    )(block_counts, x_routed, grad_out)


def solution(mesh):
    return jax.shard_map(
        per_device,
        mesh=mesh,
        in_specs=(P(None, "dp", "expert"), P(None, "dp", None), P("dp", None)),
        out_specs=P(None, "expert", None),
        check_vma=False,
    )
```

```python
import functools
import math

import jax
import jax.numpy as jnp
from jax import lax
from jax.experimental import pallas as pl
from jax.experimental.pallas import tpu as pltpu
from jax.sharding import PartitionSpec as P

D = 2048
BLK = 16
ITERS = 2


NEWTON_FIRST = 3.4445
NEWTON_SECOND = -4.775
NEWTON_THIRD = 2.0315
EPSILON = 1e-07
TILE = 256
MESH = pl.DeviceIdType.MESH


def contract_rows(left, right):
    return lax.dot_general(
        left, right, (((0,), (0,)), ((), ())), preferred_element_type=jnp.float32
    )


def gram_into(gram_ref, rows_ref, scale):
    groups, width, hidden = rows_ref.shape
    for low in range(0, hidden, TILE):
        left = rows_ref[:, :, low : low + TILE].reshape(groups * width, TILE)
        right = rows_ref[:, :, low:].reshape(groups * width, hidden - low)
        strip = contract_rows(left, right)
        if scale is not None:
            strip = strip * scale
        gram_ref[low : low + TILE, low:] = strip.astype(jnp.bfloat16)
        for other in range(low + TILE, hidden, TILE):
            block = strip[:, other - low : other - low + TILE]
            gram_ref[other : other + TILE, low : low + TILE] = block.T.astype(jnp.bfloat16)


def polynomial_into(poly_ref, gram_ref):
    hidden = gram_ref.shape[0]
    for low in range(0, hidden, TILE):
        strip = gram_ref[low : low + TILE, :]
        square = jnp.dot(strip, gram_ref[...], preferred_element_type=jnp.float32)
        poly_ref[low : low + TILE, :] = (
            NEWTON_SECOND * strip.astype(jnp.float32) + NEWTON_THIRD * square
        ).astype(jnp.bfloat16)


def turn(rows, poly_ref):
    return NEWTON_FIRST * rows.astype(jnp.float32) + jnp.dot(
        rows, poly_ref[...], preferred_element_type=jnp.float32
    )


def kernel(
    groups,
    replicas,
    parts,
    counts_ref,
    x_ref,
    g_ref,
    out_ref,
    x_all,
    g_all,
    g_raw,
    grad,
    current,
    stage,
    gram,
    poly,
    local_sem,
    x_send,
    x_recv,
    right_send,
    left_send,
    line_recv,
    out_send,
    out_recv,
    handed,
    relay_send,
):
    z = lax.axis_index("dp")
    me = lax.axis_index("expert")
    capacity = g_raw.shape[0]
    per_part = groups // parts
    last = replicas - 1
    right_exists = z < last
    left_exists = z > 0

    barrier = pltpu.get_barrier_semaphore()

    def greet(step, carry):
        peer = lax.rem(me + step, groups)
        pl.semaphore_signal(barrier, inc=1, device_id=(z, peer), device_id_type=MESH)
        return carry

    lax.fori_loop(1, groups, greet, 0)

    @pl.when(right_exists)
    def _():
        pl.semaphore_signal(barrier, inc=1, device_id=(z + 1, me), device_id_type=MESH)

    @pl.when(left_exists)
    def _():
        pl.semaphore_signal(barrier, inc=1, device_id=(z - 1, me), device_id_type=MESH)

    own_g = pltpu.make_async_copy(g_ref.at[me], g_raw, local_sem.at[0])
    own_g.start()
    own_x = pltpu.make_async_copy(x_ref.at[me], x_all.at[z, me], local_sem.at[1])
    own_x.start()

    neighbours = jnp.minimum(z, 1) + jnp.minimum(last - z, 1)
    pl.semaphore_wait(barrier, groups - 1 + neighbours)

    def x_copy(peer):
        return pltpu.make_async_remote_copy(
            src_ref=x_ref.at[peer],
            dst_ref=x_all.at[z, me],
            send_sem=x_send.at[peer],
            recv_sem=x_recv.at[me],
            device_id=(z, peer),
            device_id_type=MESH,
        )

    def x_arrival(peer):
        return pltpu.make_async_remote_copy(
            src_ref=x_ref.at[peer],
            dst_ref=x_all.at[z, peer],
            send_sem=x_send.at[peer],
            recv_sem=x_recv.at[peer],
            device_id=(z, peer),
            device_id_type=MESH,
        )

    def exchange(step, carry):
        x_copy(lax.rem(me + step, groups)).start()
        return carry

    lax.fori_loop(1, groups, exchange, 0)

    def chunk(part):
        return lax.rem(me // per_part + part - 1, parts)

    def line_copy(block, part, to, send_sem):
        if part == 0:
            view = g_all.at[block]
        else:
            view = x_all.at[block, pl.ds(chunk(part) * per_part, per_part)]
        return pltpu.make_async_remote_copy(
            src_ref=view,
            dst_ref=view,
            send_sem=send_sem.at[block, part],
            recv_sem=line_recv.at[block, part],
            device_id=(to, me),
            device_id_type=MESH,
        )

    def to_right(block, part):
        return line_copy(block, part, z + 1, right_send)

    def to_left(block, part):
        return line_copy(block, part, z - 1, left_send)

    own_g.wait()
    row_index = lax.broadcasted_iota(jnp.int32, g_raw.shape, 0)
    live = row_index < BLK * counts_ref[0, me]
    g_all[z] = jnp.where(live, g_raw[...], jnp.zeros((), g_raw.dtype))

    even = lax.rem(me, 2) == 0
    odd = jnp.logical_not(even)
    low_half = 2 * z < replicas

    def take_link(direction, exists):
        @pl.when(jnp.logical_and(odd, exists))
        def _():
            pl.semaphore_wait(handed.at[direction], 1)

    def give_link(direction, exists):
        @pl.when(jnp.logical_and(even, exists))
        def _():
            pl.semaphore_signal(
                handed.at[direction], inc=1, device_id=(z, me + 1), device_id_type=MESH
            )

    def start_right():
        take_link(0, right_exists)
        for part in range(parts + 1):

            @pl.when(right_exists)
            def _():
                to_right(z, part).start()

    def start_left():
        take_link(1, left_exists)
        for part in range(parts + 1):

            @pl.when(left_exists)
            def _():
                to_left(z, part).start()

    def own_chunk(part):
        for offset in range(per_part):
            peer = chunk(part) * per_part + offset

            @pl.when(me == peer)
            def _():
                own_x.wait()

            @pl.when(me != peer)
            def _():
                x_arrival(peer).wait_recv()

    @pl.when(even)
    def _():
        for part in range(parts + 1):
            if part > 0:
                own_chunk(part)

            @pl.when(right_exists)
            def _():
                to_right(z, part).start()

            @pl.when(left_exists)
            def _():
                to_left(z, part).start()

    @pl.when(odd)
    def _():
        for part in range(1, parts + 1):
            own_chunk(part)

        @pl.when(low_half)
        def _():
            start_right()
            start_left()

        @pl.when(jnp.logical_not(low_half))
        def _():
            start_left()
            start_right()

    for step in range(1, replicas):
        for part in range(parts + 1):

            @pl.when(z >= step)
            def _():
                to_right(z - step, part).wait_recv()

                @pl.when(right_exists)
                def _():
                    to_right(z - step, part).start()

            @pl.when(z + step <= last)
            def _():
                to_left(z + step, part).wait_recv()

                @pl.when(left_exists)
                def _():
                    to_left(z + step, part).start()

    def sent_right(step, part):
        @pl.when(jnp.logical_and(z >= step, right_exists))
        def _():
            to_right(z - step, part).wait_send()

    def sent_left(step, part):
        @pl.when(jnp.logical_and(z + step <= last, left_exists))
        def _():
            to_left(z + step, part).wait_send()

    def release_right():
        for step in range(replicas):
            for part in range(parts):
                sent_right(step, part)
        give_link(0, right_exists)

    def release_left():
        for step in range(replicas):
            for part in range(parts):
                sent_left(step, part)
        give_link(1, left_exists)

    @pl.when(jnp.logical_and(even, low_half))
    def _():
        release_right()
        release_left()

    @pl.when(jnp.logical_and(even, jnp.logical_not(low_half)))
    def _():
        release_left()
        release_right()

    hidden = g_raw.shape[1]
    width = x_ref.shape[2]
    rows = replicas * capacity

    def gradient(group, total):
        block = contract_rows(
            x_all[:, group].reshape(rows, width), g_all[...].reshape(rows, hidden)
        )
        grad[group] = block.astype(jnp.bfloat16)
        return total + jnp.sum((block * block).reshape(width // 8, 8, hidden), axis=0)

    total = lax.fori_loop(0, groups, gradient, jnp.zeros((8, hidden), jnp.float32))
    norm = jnp.sqrt(jnp.sum(total, keepdims=True)) + EPSILON
    scale = 1.0 / norm
    gram_into(gram, grad, scale * scale)
    for iteration in range(ITERS - 1):
        source = grad if iteration == 0 else current
        polynomial_into(poly, gram)

        def advance(group, carry):
            combined = turn(source[group], poly)
            if iteration == 0:
                combined = combined * scale
            current[group] = combined.astype(jnp.bfloat16)
            return carry

        lax.fori_loop(0, groups, advance, 0)
        gram_into(gram, current, None)
    polynomial_into(poly, gram)

    def out_copy(peer):
        return pltpu.make_async_remote_copy(
            src_ref=stage.at[peer],
            dst_ref=out_ref.at[me],
            send_sem=out_send.at[peer],
            recv_sem=out_recv.at[me],
            device_id=(z, peer),
            device_id_type=MESH,
        )

    def out_arrival(peer):
        return pltpu.make_async_remote_copy(
            src_ref=stage.at[peer],
            dst_ref=out_ref.at[peer],
            send_sem=out_send.at[peer],
            recv_sem=out_recv.at[peer],
            device_id=(z, peer),
            device_id_type=MESH,
        )

    def finish(peer):
        stage[peer] = (turn(current[peer], poly) * math.sqrt(D)).astype(jnp.bfloat16)

    mirror = groups - 2 - 2 * (me // 2)
    at_end = jnp.logical_or(z == 0, z == last)
    relayed = mirror + 1
    own_out = pltpu.make_async_copy(stage.at[me], out_ref.at[me], local_sem.at[0])

    def sends(step):
        if replicas < 3:
            return step >= 0
        skipped = jnp.logical_and(jnp.logical_and(odd, at_end), step < 2)
        return jnp.logical_not(skipped)

    def send_out(step, carry):
        peer = lax.rem(mirror + step, groups)

        @pl.when(sends(step))
        def _():
            finish(peer)

            @pl.when(peer != me)
            def _():
                out_copy(peer).start()

            @pl.when(peer == me)
            def _():
                own_out.start()

        return carry

    lax.fori_loop(0, groups, send_out, 0)

    def relay(to):
        return pltpu.make_async_remote_copy(
            src_ref=out_ref.at[relayed],
            dst_ref=out_ref.at[relayed],
            send_sem=relay_send.at[to],
            recv_sem=out_recv.at[relayed],
            device_id=(to * last, me),
            device_id_type=MESH,
        )

    if replicas >= 3:
        inner = jnp.logical_or(z == 1, z == last - 1)

        @pl.when(inner)
        def _():
            out_arrival(relayed).wait_recv()

        @pl.when(z == 1)
        def _():
            relay(0).start()

        @pl.when(z == last - 1)
        def _():
            relay(1).start()

    def settle(step, carry):
        peer = lax.rem(mirror + step, groups)

        @pl.when(peer != me)
        def _():
            x_copy(peer).wait_send()

            @pl.when(sends(step))
            def _():
                out_copy(peer).wait_send()

            if replicas >= 3:

                @pl.when(jnp.logical_not(jnp.logical_and(inner, peer == relayed)))
                def _():
                    out_arrival(peer).wait_recv()

            else:
                out_arrival(peer).wait_recv()

        return carry

    lax.fori_loop(0, groups, settle, 0)
    if replicas >= 3:

        @pl.when(z == 1)
        def _():
            relay(0).wait_send()

        @pl.when(z == last - 1)
        def _():
            relay(1).wait_send()

    own_out.wait()

    @pl.when(odd)
    def _():
        for step in range(replicas):
            for part in range(parts):
                sent_right(step, part)
                sent_left(step, part)

    for step in range(replicas):
        sent_right(step, parts)
        sent_left(step, parts)


def per_device(x_routed, grad_out, block_counts):
    groups = lax.axis_size("expert")
    replicas = lax.axis_size("dp")
    experts, capacity, width = x_routed.shape
    hidden = grad_out.shape[2]
    parts = 4
    dma = pltpu.SemaphoreType.DMA
    return pl.pallas_call(
        functools.partial(kernel, groups, replicas, parts),
        out_shape=jax.ShapeDtypeStruct((groups, width, hidden), jnp.bfloat16),
        in_specs=[
            pl.BlockSpec(memory_space=pltpu.SMEM),
            pl.BlockSpec(memory_space=pl.ANY),
            pl.BlockSpec(memory_space=pl.ANY),
        ],
        out_specs=pl.BlockSpec(memory_space=pl.ANY),
        scratch_shapes=[
            pltpu.VMEM((replicas, groups, capacity, width), jnp.bfloat16),
            pltpu.VMEM((replicas, capacity, hidden), jnp.bfloat16),
            pltpu.VMEM((capacity, hidden), jnp.bfloat16),
            pltpu.VMEM((groups, width, hidden), jnp.bfloat16),
            pltpu.VMEM((groups, width, hidden), jnp.bfloat16),
            pltpu.VMEM((groups, width, hidden), jnp.bfloat16),
            pltpu.VMEM((hidden, hidden), jnp.bfloat16),
            pltpu.VMEM((hidden, hidden), jnp.bfloat16),
            dma((2,)),
            dma((groups,)),
            dma((groups,)),
            dma((replicas, parts + 1)),
            dma((replicas, parts + 1)),
            dma((replicas, parts + 1)),
            dma((groups,)),
            dma((groups,)),
            pltpu.SemaphoreType.REGULAR((2,)),
            dma((2,)),
        ],
        compiler_params=pltpu.CompilerParams(
            collective_id=0, has_side_effects=True, vmem_limit_bytes=56 * 2**20
        ),
    )(block_counts, x_routed, grad_out)


def solution(mesh):
    return jax.shard_map(
        per_device,
        mesh=mesh,
        in_specs=(P(None, "dp", "expert"), P(None, "dp", None), P("dp", None)),
        out_specs=P(None, "expert", None),
        check_vma=False,
    )
```

```python
import functools
import math

import jax
import jax.numpy as jnp
from jax import lax
from jax.experimental import pallas as pl
from jax.experimental.pallas import tpu as pltpu
from jax.sharding import PartitionSpec as P

D = 2048
BLK = 16
ITERS = 2


NEWTON_FIRST = 3.4445
NEWTON_SECOND = -4.775
NEWTON_THIRD = 2.0315
EPSILON = 1e-07
TILE = 256
MESH = pl.DeviceIdType.MESH


def contract_rows(left, right):
    return lax.dot_general(
        left, right, (((0,), (0,)), ((), ())), preferred_element_type=jnp.float32
    )


def gram_into(gram_ref, rows_ref, scale):
    groups, width, hidden = rows_ref.shape
    for low in range(0, hidden, TILE):
        left = rows_ref[:, :, low : low + TILE].reshape(groups * width, TILE)
        right = rows_ref[:, :, low:].reshape(groups * width, hidden - low)
        strip = contract_rows(left, right)
        if scale is not None:
            strip = strip * scale
        gram_ref[low : low + TILE, low:] = strip.astype(jnp.bfloat16)
        for other in range(low + TILE, hidden, TILE):
            block = strip[:, other - low : other - low + TILE]
            gram_ref[other : other + TILE, low : low + TILE] = block.T.astype(jnp.bfloat16)


def polynomial_into(poly_ref, gram_ref):
    hidden = gram_ref.shape[0]
    for low in range(0, hidden, TILE):
        strip = gram_ref[low : low + TILE, :]
        square = jnp.dot(strip, gram_ref[...], preferred_element_type=jnp.float32)
        poly_ref[low : low + TILE, :] = (
            NEWTON_SECOND * strip.astype(jnp.float32) + NEWTON_THIRD * square
        ).astype(jnp.bfloat16)


def turn(rows, poly_ref):
    return NEWTON_FIRST * rows.astype(jnp.float32) + jnp.dot(
        rows, poly_ref[...], preferred_element_type=jnp.float32
    )


def kernel(
    groups,
    replicas,
    parts,
    counts_ref,
    x_ref,
    g_ref,
    out_ref,
    x_all,
    g_all,
    g_raw,
    grad,
    current,
    stage,
    gram,
    poly,
    local_sem,
    x_send,
    x_recv,
    right_send,
    left_send,
    line_recv,
    out_send,
    out_recv,
    handed,
    relay_send,
):
    z = lax.axis_index("dp")
    me = lax.axis_index("expert")
    capacity = g_raw.shape[0]
    per_part = groups // parts
    last = replicas - 1
    right_exists = z < last
    left_exists = z > 0

    barrier = pltpu.get_barrier_semaphore()

    def greet(step, carry):
        peer = lax.rem(me + step, groups)
        pl.semaphore_signal(barrier, inc=1, device_id=(z, peer), device_id_type=MESH)
        return carry

    lax.fori_loop(1, groups, greet, 0)

    @pl.when(right_exists)
    def _():
        pl.semaphore_signal(barrier, inc=1, device_id=(z + 1, me), device_id_type=MESH)

    @pl.when(left_exists)
    def _():
        pl.semaphore_signal(barrier, inc=1, device_id=(z - 1, me), device_id_type=MESH)

    own_g = pltpu.make_async_copy(g_ref.at[me], g_raw, local_sem.at[0])
    own_g.start()
    own_x = pltpu.make_async_copy(x_ref.at[me], x_all.at[z, me], local_sem.at[1])
    own_x.start()

    neighbours = jnp.minimum(z, 1) + jnp.minimum(last - z, 1)
    pl.semaphore_wait(barrier, groups - 1 + neighbours)

    def x_copy(peer):
        return pltpu.make_async_remote_copy(
            src_ref=x_ref.at[peer],
            dst_ref=x_all.at[z, me],
            send_sem=x_send.at[peer],
            recv_sem=x_recv.at[me],
            device_id=(z, peer),
            device_id_type=MESH,
        )

    def x_arrival(peer):
        return pltpu.make_async_remote_copy(
            src_ref=x_ref.at[peer],
            dst_ref=x_all.at[z, peer],
            send_sem=x_send.at[peer],
            recv_sem=x_recv.at[peer],
            device_id=(z, peer),
            device_id_type=MESH,
        )

    def exchange(step, carry):
        x_copy(lax.rem(me + step, groups)).start()
        return carry

    lax.fori_loop(1, groups, exchange, 0)

    def chunk(part):
        return lax.rem(me // per_part + part - 1, parts)

    def line_copy(block, part, to, send_sem):
        if part == 0:
            view = g_all.at[block]
        else:
            view = x_all.at[block, pl.ds(chunk(part) * per_part, per_part)]
        return pltpu.make_async_remote_copy(
            src_ref=view,
            dst_ref=view,
            send_sem=send_sem.at[block, part],
            recv_sem=line_recv.at[block, part],
            device_id=(to, me),
            device_id_type=MESH,
        )

    def to_right(block, part):
        return line_copy(block, part, z + 1, right_send)

    def to_left(block, part):
        return line_copy(block, part, z - 1, left_send)

    own_g.wait()
    row_index = lax.broadcasted_iota(jnp.int32, g_raw.shape, 0)
    live = row_index < BLK * counts_ref[0, me]
    g_all[z] = jnp.where(live, g_raw[...], jnp.zeros((), g_raw.dtype))

    even = lax.rem(me, 2) == 0
    odd = jnp.logical_not(even)
    low_half = 2 * z < replicas

    def take_link(direction, exists):
        @pl.when(jnp.logical_and(odd, exists))
        def _():
            pl.semaphore_wait(handed.at[direction], 1)

    def give_link(direction, exists):
        @pl.when(jnp.logical_and(even, exists))
        def _():
            pl.semaphore_signal(
                handed.at[direction], inc=1, device_id=(z, me + 1), device_id_type=MESH
            )

    def start_right():
        take_link(0, right_exists)
        for part in range(parts + 1):

            @pl.when(right_exists)
            def _():
                to_right(z, part).start()

    def start_left():
        take_link(1, left_exists)
        for part in range(parts + 1):

            @pl.when(left_exists)
            def _():
                to_left(z, part).start()

    def own_chunk(part):
        for offset in range(per_part):
            peer = chunk(part) * per_part + offset

            @pl.when(me == peer)
            def _():
                own_x.wait()

            @pl.when(me != peer)
            def _():
                x_arrival(peer).wait_recv()

    @pl.when(even)
    def _():
        for part in range(parts + 1):
            if part > 0:
                own_chunk(part)

            @pl.when(right_exists)
            def _():
                to_right(z, part).start()

            @pl.when(left_exists)
            def _():
                to_left(z, part).start()

    @pl.when(odd)
    def _():
        for part in range(1, parts + 1):
            own_chunk(part)

        @pl.when(low_half)
        def _():
            start_right()
            start_left()

        @pl.when(jnp.logical_not(low_half))
        def _():
            start_left()
            start_right()

    for step in range(1, replicas):
        for part in range(parts + 1):

            @pl.when(z >= step)
            def _():
                to_right(z - step, part).wait_recv()

                @pl.when(right_exists)
                def _():
                    to_right(z - step, part).start()

            @pl.when(z + step <= last)
            def _():
                to_left(z + step, part).wait_recv()

                @pl.when(left_exists)
                def _():
                    to_left(z + step, part).start()

    def sent_right(step, part):
        @pl.when(jnp.logical_and(z >= step, right_exists))
        def _():
            to_right(z - step, part).wait_send()

    def sent_left(step, part):
        @pl.when(jnp.logical_and(z + step <= last, left_exists))
        def _():
            to_left(z + step, part).wait_send()

    def release_right():
        for step in range(replicas):
            for part in range(parts):
                sent_right(step, part)
        give_link(0, right_exists)

    def release_left():
        for step in range(replicas):
            for part in range(parts):
                sent_left(step, part)
        give_link(1, left_exists)

    @pl.when(jnp.logical_and(even, low_half))
    def _():
        release_right()
        release_left()

    @pl.when(jnp.logical_and(even, jnp.logical_not(low_half)))
    def _():
        release_left()
        release_right()

    hidden = g_raw.shape[1]
    width = x_ref.shape[2]
    rows = replicas * capacity

    def gradient(group, total):
        block = contract_rows(
            x_all[:, group].reshape(rows, width), g_all[...].reshape(rows, hidden)
        )
        grad[group] = block.astype(jnp.bfloat16)
        return total + jnp.sum((block * block).reshape(width // 8, 8, hidden), axis=0)

    total = lax.fori_loop(0, groups, gradient, jnp.zeros((8, hidden), jnp.float32))
    norm = jnp.sqrt(jnp.sum(total, keepdims=True)) + EPSILON
    scale = 1.0 / norm
    gram_into(gram, grad, scale * scale)
    for iteration in range(ITERS - 1):
        source = grad if iteration == 0 else current
        polynomial_into(poly, gram)

        def advance(group, carry):
            combined = turn(source[group], poly)
            if iteration == 0:
                combined = combined * scale
            current[group] = combined.astype(jnp.bfloat16)
            return carry

        lax.fori_loop(0, groups, advance, 0)
        gram_into(gram, current, None)
    polynomial_into(poly, gram)

    def out_copy(peer):
        return pltpu.make_async_remote_copy(
            src_ref=stage.at[peer],
            dst_ref=out_ref.at[me],
            send_sem=out_send.at[peer],
            recv_sem=out_recv.at[me],
            device_id=(z, peer),
            device_id_type=MESH,
        )

    def out_arrival(peer):
        return pltpu.make_async_remote_copy(
            src_ref=stage.at[peer],
            dst_ref=out_ref.at[peer],
            send_sem=out_send.at[peer],
            recv_sem=out_recv.at[peer],
            device_id=(z, peer),
            device_id_type=MESH,
        )

    def finish(peer):
        stage[peer] = (turn(current[peer], poly) * math.sqrt(D)).astype(jnp.bfloat16)

    mirror = groups - 2 - 2 * (me // 2)
    at_end = jnp.logical_or(z == 0, z == last)
    relayed = mirror + 1
    own_out = pltpu.make_async_copy(stage.at[me], out_ref.at[me], local_sem.at[0])

    def sends(step):
        if replicas < 3:
            return step >= 0
        skipped = jnp.logical_and(jnp.logical_and(odd, at_end), step < 2)
        return jnp.logical_not(skipped)

    def send_out(step, carry):
        peer = lax.rem(mirror + step, groups)

        @pl.when(sends(step))
        def _():
            finish(peer)

            @pl.when(peer != me)
            def _():
                out_copy(peer).start()

            @pl.when(peer == me)
            def _():
                own_out.start()

        return carry

    lax.fori_loop(0, groups, send_out, 0)

    def relay(to):
        return pltpu.make_async_remote_copy(
            src_ref=out_ref.at[relayed],
            dst_ref=out_ref.at[relayed],
            send_sem=relay_send.at[to],
            recv_sem=out_recv.at[relayed],
            device_id=(to * last, me),
            device_id_type=MESH,
        )

    if replicas >= 3:
        inner = jnp.logical_or(z == 1, z == last - 1)

        @pl.when(inner)
        def _():
            out_arrival(relayed).wait_recv()

        @pl.when(z == 1)
        def _():
            relay(0).start()

        @pl.when(z == last - 1)
        def _():
            relay(1).start()

    def settle(step, carry):
        peer = lax.rem(mirror + step, groups)

        @pl.when(peer != me)
        def _():
            x_copy(peer).wait_send()

            @pl.when(sends(step))
            def _():
                out_copy(peer).wait_send()

            if replicas >= 3:

                @pl.when(jnp.logical_not(jnp.logical_and(inner, peer == relayed)))
                def _():
                    out_arrival(peer).wait_recv()

            else:
                out_arrival(peer).wait_recv()

        return carry

    lax.fori_loop(0, groups, settle, 0)
    if replicas >= 3:

        @pl.when(z == 1)
        def _():
            relay(0).wait_send()

        @pl.when(z == last - 1)
        def _():
            relay(1).wait_send()

    own_out.wait()

    @pl.when(odd)
    def _():
        for step in range(replicas):
            for part in range(parts):
                sent_right(step, part)
                sent_left(step, part)

    for step in range(replicas):
        sent_right(step, parts)
        sent_left(step, parts)


def per_device(x_routed, grad_out, block_counts):
    groups = lax.axis_size("expert")
    replicas = lax.axis_size("dp")
    experts, capacity, width = x_routed.shape
    hidden = grad_out.shape[2]
    parts = 4
    dma = pltpu.SemaphoreType.DMA
    return pl.pallas_call(
        functools.partial(kernel, groups, replicas, parts),
        out_shape=pltpu.VMEM((groups, width, hidden), jnp.bfloat16),
        in_specs=[
            pl.BlockSpec(memory_space=pltpu.SMEM),
            pl.BlockSpec(memory_space=pl.ANY),
            pl.BlockSpec(memory_space=pl.ANY),
        ],
        out_specs=pl.BlockSpec(memory_space=pltpu.VMEM),
        scratch_shapes=[
            pltpu.VMEM((replicas, groups, capacity, width), jnp.bfloat16),
            pltpu.VMEM((replicas, capacity, hidden), jnp.bfloat16),
            pltpu.VMEM((capacity, hidden), jnp.bfloat16),
            pltpu.VMEM((groups, width, hidden), jnp.bfloat16),
            pltpu.VMEM((groups, width, hidden), jnp.bfloat16),
            pltpu.VMEM((groups, width, hidden), jnp.bfloat16),
            pltpu.VMEM((hidden, hidden), jnp.bfloat16),
            pltpu.VMEM((hidden, hidden), jnp.bfloat16),
            dma((2,)),
            dma((groups,)),
            dma((groups,)),
            dma((replicas, parts + 1)),
            dma((replicas, parts + 1)),
            dma((replicas, parts + 1)),
            dma((groups,)),
            dma((groups,)),
            pltpu.SemaphoreType.REGULAR((2,)),
            dma((2,)),
        ],
        compiler_params=pltpu.CompilerParams(
            collective_id=0, has_side_effects=True, vmem_limit_bytes=57 * 2**20
        ),
    )(block_counts, x_routed, grad_out)


def solution(mesh):
    return jax.shard_map(
        per_device,
        mesh=mesh,
        in_specs=(P(None, "dp", "expert"), P(None, "dp", None), P("dp", None)),
        out_specs=P(None, "expert", None),
        check_vma=False,
    )
```
